32 devices in a mesh: dp: 8 (over z, y), cent: 4 (over x, core).
Axes of the slice: x: 2, y: 2, z: 4, core: 2. Of those that a mesh axis runs over, the one named last changes fastest.
Arguments:
- clip_data: bfloat16 [4096, 4, 16, 192], P(('dp', 'cent')), may hold values from -6 to 6
- frame_counts: int32 [32, 128], P(('dp', 'cent')), may hold values from 1 to 4, 320 in all within a row
- send_list: int32 [32, 128], P(('dp', 'cent')), may hold values from 0 to 127, each once within a row
- cluster_ids: int32 [32, 128], P(('dp', 'cent')), may hold values from 0 to 37531, as said below
- expand_weight: bfloat16 [2, 192, 432], replicated, may hold values from -0.4375 to 0.4375
- depth_kernel: bfloat16 [2, 27, 432], replicated, may hold values from -1.25 to 1.25
- reduce_weight: bfloat16 [2, 432, 192], replicated, may hold values from -0.3125 to 0.3125
- head_weight: bfloat16 [192, 1024], replicated, may hold values from -0.4375 to 0.4375
- centroids: bfloat16 [50000, 1024], P('cent'), may hold values from -6 to 6
Outputs:
- embeddings: bfloat16 [4096, 1024], P(('dp', 'cent'))
- nearest: float32 [4096], P(('dp', 'cent'))
- own_sim: float32 [4096], P(('dp', 'cent'))
- peer_sim: float32 [4096], P(('dp', 'cent'))
The draws below stay inside these ranges and needn't reach their ends.
Inputs may be any that keep to these rules, and one draw needn't show every extreme that they name: `cluster_ids`: cluster id q is owned by the device with dp index (q % 12500) % 8 and cent index q // 12500. The clips of one device name at most 16 clusters of one owner, and in every draw one owner gets exactly 16 from every device. Only ids with q % 12500 < 32 occur.
All inputs are finite; a program needn't handle non-finite values.
Results may differ from the reference program's by a relative error of at most 0.014.
Values may be sent and summed in bfloat16 or wider, within the bound.
A program may use at most 128 MiB of HBM per device.

```python
import math
import jax
import jax.numpy as jnp
import numpy as np
from jax import lax

C = 192
E = 432
D = 1024
K = 50000
LAYERS = 2
FR = 4
SIDE = 4
CL = 128
OWNERS = 32
CLIPS = 4096
KP = 12500
DP_SHARDS = 8
CAP = 16
GROUPS = 4
N_DP = 8
N_CENT = 4


def draw_cluster_ids(key, part):
    busiest = jax.random.randint(jax.random.fold_in(key, 1), (), 0, OWNERS)
    cent_count = K // KP

    def one_device(device):
        device_key = jax.random.fold_in(key, device + 100)
        tokens = jax.random.permutation(jax.random.fold_in(device_key, 2), CAP * (OWNERS - 1))
        ranked = tokens[:CL - CAP] // CAP
        others = (ranked + (ranked >= busiest).astype(jnp.int32)).astype(jnp.int32)
        listed = jnp.concatenate([jnp.full((CAP,), busiest, jnp.int32), others])
        shuffled_order = jax.random.permutation(jax.random.fold_in(device_key, 3), CL)
        targets = listed[shuffled_order]
        groups = jax.random.randint(jax.random.fold_in(device_key, 4), (CL,), 0, GROUPS)
        dp_part = targets // cent_count
        cent_part = targets % cent_count
        return (cent_part * KP + groups * DP_SHARDS + dp_part).astype(jnp.int32)
    return jax.vmap(one_device)(jnp.arange(OWNERS, dtype=jnp.int32))


def block_levels(own_key, extent, pieces, least, top_value):
    gain = 1.0
    for axis_at, shards_of in pieces:
        heights = jax.random.uniform(jax.random.fold_in(jax.random.fold_in(own_key, 6), axis_at), (shards_of,), jnp.float32, least / len(pieces), top_value / len(pieces))
        gain = gain * jnp.repeat(jnp.exp(heights), extent[axis_at] // shards_of).reshape((-1,) + (1,) * (len(extent) - 1 - axis_at))
    return gain


def split_up(count, total, limit, skew):
    loads = [(1 << 20) // math.isqrt(grade ** skew) + 1 for grade in range(2, count + 1)]
    surplus, counts = total - limit - (count - 1), [1] * (count - 1)
    while surplus > 0:
        movable = [i for i in range(count - 1) if counts[i] < limit]
        mass, left = sum([loads[i] for i in movable]), surplus
        for i in movable:
            extra = min(limit - counts[i], max(1, left * loads[i] // mass), surplus)
            counts[i] = counts[i] + extra
            surplus = surplus - extra
    return np.array([limit] + counts)


def ragged_sizes(key, number_of, total, limit, slope):
    if number_of == 2:
        one = jax.random.randint(key, (), max(1, total - limit), min(limit, total - 1) + 1)
        return jnp.stack([one, total - one])
    lengths = jnp.asarray(split_up(number_of, total, limit, slope), jnp.int32)
    twos = (number_of - 1) // 2
    source_of, receiver = lengths[1:1 + 2 * twos:2], lengths[2:2 + 2 * twos:2]
    room = jnp.minimum(source_of - 1, limit - receiver)
    moved = jax.random.randint(jax.random.fold_in(key, 1), (twos,), 0, 1 << 20) % (room + 1)
    lengths = lengths.at[1:1 + 2 * twos:2].set(source_of - moved).at[2:2 + 2 * twos:2].set(receiver + moved)
    return lengths[jax.random.permutation(jax.random.fold_in(key, 2), number_of)]


def centred(key, dims, deviation, bound, pieces=(), held_as=jnp.bfloat16):
    values = deviation * jax.random.normal(key, dims, jnp.float32)
    if pieces:
        values = values * block_levels(key, dims, pieces, -0.22, 0.18)
    return jnp.clip(values, -bound, bound).astype(held_as)


def setup_inputs(seed: int = 0) -> dict:
    splits = jax.random.split(jax.random.key(seed), 10)
    return {
        "clip_data": centred(splits[0], (CLIPS, FR, SIDE * SIDE, C), 1.0, 6.0, ((0, 32),)),
        "frame_counts": jax.vmap(lambda own: ragged_sizes(own, CL, CL * FR * 5 // 8, FR, 2))(jax.random.split(splits[1], OWNERS)).reshape((OWNERS, CL)).astype(jnp.int32),
        "send_list": jax.vmap(lambda own: jax.random.permutation(own, CL))(jax.random.split(splits[2], OWNERS)).reshape((OWNERS, CL)).astype(jnp.int32),
        "cluster_ids": draw_cluster_ids(jax.random.fold_in(splits[9], 71), 0),
        "expand_weight": centred(splits[4], (LAYERS, C, E), C ** -0.5, 0.4375),
        "depth_kernel": centred(splits[5], (LAYERS, 27, E), 27 ** -0.5, 1.25),
        "reduce_weight": centred(splits[6], (LAYERS, E, C), E ** -0.5, 0.3125),
        "head_weight": centred(splits[7], (C, D), C ** -0.5, 0.4375),
        "centroids": centred(splits[8], (K, D), 1.0, 6.0, ((0, 4),)),
    }


def depthwise(hidden, kernel):
    frame_count = hidden.shape[1]
    padded = jnp.pad(hidden, ((0, 0), (1, 1), (1, 1), (1, 1), (0, 0)))
    accumulated = jnp.zeros_like(hidden)
    for shift_t in range(3):
        for shift_y in range(3):
            for shift_x in range(3):
                accumulated = accumulated + kernel[9 * shift_t + 3 * shift_y + shift_x] * padded[:, shift_t:shift_t + frame_count, shift_y:shift_y + SIDE, shift_x:shift_x + SIDE, :]
    return accumulated

def embed_clips(clip_block, length_values, expand_weight, depth_kernel, reduce_weight, head_weight):
    clip_count, frame_count, positions, channels = clip_block.shape
    frame_mask = (jnp.arange(frame_count, dtype=jnp.float32)[None, :] < length_values[:, None]).astype(jnp.float32)
    mask_four = frame_mask[:, :, None, None]
    features = clip_block * mask_four.astype(jnp.bfloat16)
    for layer_index in range(expand_weight.shape[0]):
        hidden = jax.nn.relu(jnp.dot(features.reshape(-1, channels), expand_weight[layer_index], preferred_element_type=jnp.float32))
        expanded = hidden.shape[-1]
        hidden = hidden.reshape(clip_count, frame_count, SIDE, SIDE, expanded) * frame_mask[:, :, None, None, None]
        mixed = depthwise(hidden, depth_kernel[layer_index].astype(jnp.float32))
        activated = (mixed * jax.nn.sigmoid(mixed)).astype(jnp.bfloat16)
        branch = jnp.dot(activated.reshape(-1, expanded), reduce_weight[layer_index], preferred_element_type=jnp.float32)
        branch = branch.reshape(clip_count, frame_count, positions, channels)
        features = (features.astype(jnp.float32) + branch * mask_four).astype(jnp.bfloat16)
    pooled = (lax.optimization_barrier(jnp.sum(features.astype(jnp.float32), axis=(1, 2))) / (length_values * positions)[:, None]).astype(jnp.bfloat16)
    projected = jnp.dot(pooled, head_weight, preferred_element_type=jnp.float32)
    return (projected * lax.rsqrt(lax.optimization_barrier(jnp.sum(projected * projected, axis=1, keepdims=True)) + 1e-06)).astype(jnp.bfloat16)

def reference(clip_data, frame_counts, send_list, cluster_ids, expand_weight, depth_kernel, reduce_weight, head_weight, centroids):
    owner_total = N_DP * N_CENT
    total_rows = owner_total * CL
    source = jnp.arange(total_rows, dtype=jnp.int32)
    device = source // CL
    dp_index = device // N_CENT
    cent_index = device % N_CENT
    destination = send_list.reshape(-1).astype(jnp.int32)
    peer_index = destination % N_DP
    target_row = (peer_index * N_CENT + cent_index) * CL + destination - peer_index + dp_index
    shuffled = jnp.zeros_like(clip_data).at[target_row].set(clip_data)
    shuffled_counts = jnp.zeros((total_rows,), jnp.int32).at[target_row].set(frame_counts.reshape(-1).astype(jnp.int32))
    blocks = total_rows // 64

    def embed_block(pair):
        return embed_clips(pair[0], pair[1].astype(jnp.float32), expand_weight, depth_kernel, reduce_weight, head_weight)
    embeddings = lax.map(embed_block, (shuffled.reshape((blocks, 64) + clip_data.shape[1:]), shuffled_counts.reshape(blocks, 64)))
    embeddings = embeddings.reshape(total_rows, -1)

    def block_nearest(block_rows):
        scores = lax.dot_general(block_rows, centroids, (((1,), (1,)), ((), ())), preferred_element_type=jnp.float32)
        return lax.optimization_barrier(jnp.max(scores, axis=1))
    nearest = lax.map(block_nearest, embeddings.reshape(total_rows // 512, 512, -1)).reshape(-1)
    flat_ids = cluster_ids.reshape(-1).astype(jnp.int32)
    own_sim = lax.optimization_barrier(jnp.sum(embeddings.astype(jnp.float32) * centroids[flat_ids].astype(jnp.float32), axis=1))
    panel_index = flat_ids % KP
    target = panel_index % N_DP * N_CENT + flat_ids // KP
    capacity_all = owner_total * CAP

    def owner_peers(owner_id):
        ranking = jnp.where(target == owner_id, total_rows - source, 0)
        top_values, members = lax.top_k(ranking, capacity_all)
        filled = top_values > 0
        member_vectors = embeddings[members]
        member_ids = flat_ids[members]
        similarity = lax.dot_general(member_vectors, member_vectors, (((1,), (1,)), ((), ())), preferred_element_type=jnp.float32)
        slots = jnp.arange(capacity_all, dtype=jnp.int32)
        same_cluster = (member_ids[:, None] == member_ids[None, :]) & filled[:, None] & filled[None, :] & (slots[:, None] != slots[None, :])
        best_peer = lax.optimization_barrier(jnp.max(jnp.where(same_cluster, similarity, -1.0), axis=1))
        return (best_peer, jnp.where(filled, members, total_rows))
    peer_values, places = lax.map(owner_peers, jnp.arange(owner_total, dtype=jnp.int32))
    peer_sim = jnp.zeros((total_rows,), jnp.float32).at[places.reshape(-1)].set(peer_values.reshape(-1), mode='drop')
    return (embeddings, nearest, own_sim, peer_sim)
```

```python
import functools

import jax
import jax.numpy as jnp
from jax import lax
from jax.experimental import pallas as pl
from jax.experimental.pallas import tpu as pltpu
from jax.sharding import PartitionSpec as P

SIDE = 4
GROUPS = 4
ROWS = 16
F32 = jnp.float32
BF16 = jnp.bfloat16


def embed_kernel(
    order_ref,
    most_ref,
    clip_ref,
    count_ref,
    place_ref,
    expand_ref,
    depth_ref,
    reduce_ref,
    head_ref,
    out_ref,
    arrived,
    x,
    hidden,
    activated,
    pooled,
    taps,
    sems,
):
    clips, frames, positions, channels = clip_ref.shape
    layers, tap_count, expanded = depth_ref.shape
    blocks = clips // ROWS
    flat = positions * ROWS

    def fetch(i, carry):
        pltpu.make_async_copy(
            clip_ref.at[order_ref[i]], arrived.at[i], sems.at[i // ROWS]
        ).start()
        return carry

    lax.fori_loop(0, clips, fetch, 0)

    for layer in range(layers):
        rows = depth_ref[layer].astype(F32)
        for t in range(tap_count):
            taps[layer, t] = jnp.broadcast_to(rows[t : t + 1], (ROWS, expanded)).astype(BF16)

    to_row = lax.broadcasted_iota(jnp.int32, (flat, flat), 0)
    from_row = lax.broadcasted_iota(jnp.int32, (flat, flat), 1)
    turn = jnp.where(
        from_row == (to_row % ROWS) * positions + to_row // ROWS, 1.0, 0.0
    ).astype(BF16)
    lanes = [(at, min(at + 128, expanded)) for at in range(0, expanded, 128)]

    def convolve(layer, f, shifts):
        for lo, hi in lanes:
            for y in range(SIDE):
                sums = [None] * SIDE
                for a in shifts:
                    for b in range(3):
                        if not 0 <= y + b - 1 < SIDE:
                            continue
                        line = [
                            hidden[f + a - 1, (y + b - 1) * SIDE + z, :, lo:hi]
                            for z in range(SIDE)
                        ]
                        weights = [taps[layer, 9 * a + 3 * b + g, :, lo:hi] for g in range(3)]
                        for z in range(SIDE):
                            for g in range(3):
                                if 0 <= z + g - 1 < SIDE:
                                    term = weights[g] * line[z + g - 1]
                                    sums[z] = term if sums[z] is None else sums[z] + term
                for z in range(SIDE):
                    half = 0.5 * sums[z].astype(F32)
                    activated[y * SIDE + z, :, lo:hi] = (half + half * jnp.tanh(half)).astype(BF16)

    def block(b, carry):
        most = most_ref[b]
        first = pl.multiple_of(b * ROWS, ROWS)
        pltpu.make_async_copy(
            clip_ref.at[pl.ds(0, ROWS)], arrived.at[pl.ds(first, ROWS)], sems.at[b]
        ).wait()
        counts = count_ref[pl.ds(first, ROWS), :]

        def mask(f, width):
            wide = jnp.broadcast_to(counts, (ROWS, width))
            return jnp.where(wide > f.astype(F32), 1.0, 0.0)

        def load(f, carry):
            raw = arrived[pl.ds(first, ROWS), f].reshape(flat, channels)
            turned = jnp.dot(turn, raw, preferred_element_type=F32)
            x[f] = (turned.reshape(positions, ROWS, channels) * mask(f, channels)[None]).astype(BF16)
            return carry

        lax.fori_loop(0, most, load, 0)

        def layer_step(layer, carry):
            def expand(f, carry):
                wide = jnp.dot(
                    x[f].reshape(flat, channels), expand_ref[layer], preferred_element_type=F32
                )
                wide = jnp.maximum(wide, 0.0).astype(BF16).reshape(positions, ROWS, expanded)
                hidden[f] = wide * mask(f, expanded).astype(BF16)[None]
                return carry

            lax.fori_loop(0, most, expand, 0)

            def mix(f, carry):
                has_last, has_next = f > 0, f < most - 1
                for last in (False, True):
                    for following in (False, True):
                        shifts = ([0] if last else []) + [1] + ([2] if following else [])
                        chosen = jnp.logical_and(has_last == last, has_next == following)
                        pl.when(chosen)(functools.partial(convolve, layer, f, shifts))
                branch = jnp.dot(
                    activated[...].reshape(flat, expanded),
                    reduce_ref[layer],
                    preferred_element_type=F32,
                ).reshape(positions, ROWS, channels)
                x[f] = (x[f].astype(F32) + branch * mask(f, channels)[None]).astype(BF16)
                return carry

            lax.fori_loop(0, most, mix, 0)
            return carry

        lax.fori_loop(0, layers, layer_step, 0)

        total = lax.fori_loop(
            0,
            most,
            lambda f, total: total + jnp.sum(x[f].astype(F32), axis=0),
            jnp.zeros((ROWS, channels), F32),
        )
        mean = total / (jnp.broadcast_to(counts, (ROWS, channels)) * positions)
        pooled[pl.ds(first, ROWS), :] = mean.astype(BF16)
        return carry

    lax.fori_loop(0, blocks, block, 0)

    projected = jnp.dot(pooled[...], head_ref[...], preferred_element_type=F32)
    square = jnp.sum(projected * projected, axis=1, keepdims=True)
    vectors = (projected * lax.rsqrt(square + 1e-06)).astype(BF16)
    slots = lax.broadcasted_iota(jnp.int32, (clips, clips), 0)
    chosen = jnp.where(slots == place_ref[...], 1.0, 0.0).astype(BF16)
    out_ref[...] = jnp.dot(chosen, vectors, preferred_element_type=F32).astype(BF16)


def embed(clip_data, counts, places, expand_weight, depth_kernel, reduce_weight, head_weight):
    clips, frames, positions, channels = clip_data.shape
    layers, tap_count, expanded = depth_kernel.shape
    blocks = clips // ROWS
    slots = jnp.arange(clips, dtype=jnp.int32)
    ahead = (counts[None, :] > counts[:, None]) | (
        (counts[None, :] == counts[:, None]) & (slots[None, :] < slots[:, None])
    )
    rank = jnp.sum(ahead.astype(jnp.int32), axis=1)
    at_rank = rank[None, :] == slots[:, None]

    def ranked(values):
        return jnp.sum(jnp.where(at_rank, values[None, :], 0), axis=1)

    order, sorted_counts, sorted_places = ranked(slots), ranked(counts), ranked(places)
    vmem = pl.BlockSpec(memory_space=pltpu.VMEM)
    smem = pl.BlockSpec(memory_space=pltpu.SMEM)
    return pl.pallas_call(
        embed_kernel,
        out_shape=jax.ShapeDtypeStruct((clips, head_weight.shape[1]), BF16),
        in_specs=[smem, smem, pl.BlockSpec(memory_space=pl.ANY)] + [vmem] * 6,
        out_specs=vmem,
        scratch_shapes=[
            pltpu.VMEM((clips, frames, positions, channels), BF16),
            pltpu.VMEM((frames, positions, ROWS, channels), BF16),
            pltpu.VMEM((frames, positions, ROWS, expanded), BF16),
            pltpu.VMEM((positions, ROWS, expanded), BF16),
            pltpu.VMEM((clips, channels), BF16),
            pltpu.VMEM((layers, tap_count, ROWS, expanded), BF16),
            pltpu.SemaphoreType.DMA((blocks,)),
        ],
        compiler_params=pltpu.CompilerParams(vmem_limit_bytes=40 << 20),
        name="embed_clips",
    )(
        order,
        sorted_counts[::ROWS],
        clip_data,
        sorted_counts.astype(F32)[:, None],
        sorted_places[None, :],
        expand_weight,
        depth_kernel,
        reduce_weight,
        head_weight,
    )


def score_kernel(panel_size, known, part, rows_ref, label_ref, panel_ref, out_ref, best):
    step = pl.program_id(0)
    tile = panel_ref.shape[0]
    rows = rows_ref.shape[0]

    @pl.when(step == 0)
    def _():
        best[...] = jnp.full(best.shape, -jnp.inf, F32)

    for at in range(0, tile, part):
        scores = lax.dot_general(
            panel_ref[at : at + part, :],
            rows_ref[...],
            (((1,), (1,)), ((), ())),
            preferred_element_type=F32,
        )
        if at == 0:

            @pl.when(step == 0)
            def _():
                index = lax.broadcasted_iota(jnp.int32, (known, rows), 0)
                own = jnp.where(index == label_ref[...], scores[:known], -jnp.inf)
                out_ref[1:2, :] = jnp.max(own, axis=0, keepdims=True)

        place = step * tile + at + lax.broadcasted_iota(jnp.int32, scores.shape, 0)
        scores = jnp.where(place < panel_size, scores, -jnp.inf)
        best[...] = jnp.maximum(best[...], jnp.max(scores.reshape(part // 8, 8, rows), axis=0))

    @pl.when(step == pl.num_programs(0) - 1)
    def _():
        out_ref[0:1, :] = jnp.max(best[...], axis=0, keepdims=True)


def panel_scores(rows, labels, centroids, known):
    panel_size, width = centroids.shape
    count = rows.shape[0]
    tile, part = 1024, 256
    return pl.pallas_call(
        functools.partial(score_kernel, panel_size, known, part),
        out_shape=jax.ShapeDtypeStruct((2, count), F32),
        grid=(pl.cdiv(panel_size, tile),),
        in_specs=[
            pl.BlockSpec((count, width), lambda i: (0, 0)),
            pl.BlockSpec((1, count), lambda i: (0, 0)),
            pl.BlockSpec((tile, width), lambda i: (i, 0)),
        ],
        out_specs=pl.BlockSpec((2, count), lambda i: (0, 0)),
        scratch_shapes=[pltpu.VMEM((8, count), F32)],
        compiler_params=pltpu.CompilerParams(vmem_limit_bytes=40 << 20),
        name="panel_scores",
    )(rows, labels, centroids)


def local(
    clip_data,
    frame_counts,
    send_list,
    cluster_ids,
    expand_weight,
    depth_kernel,
    reduce_weight,
    head_weight,
    centroids,
):
    n_dp = lax.axis_size("dp")
    n_cent = lax.axis_size("cent")
    both = ("dp", "cent")
    clip_count = clip_data.shape[0]
    panel_size = centroids.shape[0]
    per_peer = clip_count // n_dp
    owner_total = n_dp * n_cent
    capacity = max(2, 4 * clip_count // owner_total)
    slot_total = owner_total * capacity
    me = lax.axis_index("dp") * n_cent + lax.axis_index("cent")

    def owner_of(ids):
        return ids % panel_size % n_dp * n_cent + ids // panel_size

    every_id = lax.all_gather(cluster_ids[0], both, axis=0)
    group_ids = lax.dynamic_slice_in_dim(
        every_id, lax.axis_index("dp") * n_cent, n_cent, axis=0
    ).reshape(1, n_cent * clip_count)
    labels = jnp.where(
        group_ids // panel_size == lax.axis_index("cent"), group_ids % panel_size, -1
    )
    mine = owner_of(every_id) == me
    slots = jnp.arange(clip_count, dtype=jnp.int32)
    before = (slots[:, None] < slots[None, :]).astype(BF16)
    rank_here = jnp.dot(mine.astype(BF16), before, preferred_element_type=F32).astype(jnp.int32)
    seats = jnp.arange(capacity, dtype=jnp.int32)
    seated = mine[:, None, :] & (rank_here[:, None, :] == seats[None, :, None])
    member_ids = (
        jnp.sum(jnp.where(seated, every_id[:, None, :] + 1, 0), axis=2).reshape(slot_total) - 1
    )

    given = cluster_ids[0]
    target = owner_of(given)
    earlier = (target[:, None] == target[None, :]) & (slots[None, :] < slots[:, None])
    seat = target * capacity + jnp.sum(earlier.astype(jnp.int32), axis=1)
    places = send_list[0] % n_dp * per_peer + send_list[0] // n_dp

    outgoing = embed(
        clip_data,
        frame_counts[0],
        places,
        expand_weight,
        depth_kernel,
        reduce_weight,
        head_weight,
    )
    width = outgoing.shape[1]
    vectors = (
        lax.all_to_all(
            outgoing.reshape(n_dp, per_peer, width), "dp", split_axis=0, concat_axis=0, tiled=True
        )
        .transpose(1, 0, 2)
        .reshape(clip_count, width)
    )
    block_rows = lax.all_gather(vectors, "cent", axis=0, tiled=True)

    at_seat = jnp.arange(slot_total, dtype=jnp.int32)[:, None] == seat[None, :]
    sent = jnp.dot(at_seat.astype(BF16), vectors, preferred_element_type=F32).astype(BF16)
    members = lax.all_to_all(
        sent.reshape(owner_total, capacity, width), both, split_axis=0, concat_axis=0, tiled=True
    ).reshape(slot_total, width)

    partial = panel_scores(block_rows, labels, centroids, GROUPS * n_dp)
    partial = partial.reshape(2, n_cent, clip_count).transpose(1, 0, 2)
    partial = lax.all_to_all(partial, "cent", split_axis=0, concat_axis=0, tiled=True)
    nearest, own_sim = jnp.max(partial, axis=0)

    similarity = jnp.einsum("rd,td->rt", members, members, preferred_element_type=F32)
    index = jnp.arange(slot_total, dtype=jnp.int32)
    same_cluster = (
        (member_ids[:, None] == member_ids[None, :])
        & (member_ids >= 0)[:, None]
        & (index[:, None] != index[None, :])
    )
    peer_values = jnp.max(jnp.where(same_cluster, similarity, -1.0), axis=1)
    back = lax.all_to_all(
        peer_values.reshape(owner_total, capacity), both, split_axis=0, concat_axis=0, tiled=True
    ).reshape(slot_total)
    peer_sim = jnp.max(jnp.where(at_seat, back[:, None], -1.0), axis=0)
    return (vectors, nearest, own_sim, peer_sim)


def solution(mesh):
    placed = (
        P(("dp", "cent"), None, None, None),
        P(("dp", "cent"), None),
        P(("dp", "cent"), None),
        P(("dp", "cent"), None),
        P(),
        P(),
        P(),
        P(),
        P("cent", None),
    )
    return jax.shard_map(
        local,
        mesh=mesh,
        in_specs=placed,
        out_specs=(
            P(("dp", "cent"), None),
            P(("dp", "cent")),
            P(("dp", "cent")),
            P(("dp", "cent")),
        ),
        check_vma=False,
    )
```

```python
import functools

import jax
import jax.numpy as jnp
from jax import lax
from jax.experimental import pallas as pl
from jax.experimental.pallas import tpu as pltpu
from jax.sharding import PartitionSpec as P

SIDE = 4
GROUPS = 4
ROWS = 16
F32 = jnp.float32
BF16 = jnp.bfloat16


def embed_kernel(
    most_ref,
    order_ref,
    clip_ref,
    count_ref,
    place_ref,
    expand_ref,
    depth_ref,
    reduce_ref,
    head_ref,
    out_ref,
    x,
    hidden,
    activated,
    pooled,
    taps,
):
    frames, positions, channels, clips = clip_ref.shape
    layers, tap_count, expanded = depth_ref.shape
    blocks = clips // ROWS
    flat = positions * ROWS

    clip_of = lax.broadcasted_iota(jnp.int32, (clips, clips), 1)
    by_count = jnp.where(clip_of == order_ref[...], 1.0, 0.0).astype(BF16)
    every_count = jnp.broadcast_to(count_ref[...], (clips, channels))

    def load(f, carry):
        kept = jnp.where(every_count > f.astype(F32), 1.0, 0.0)

        def place(p, carry):
            ranked = lax.dot_general(
                by_count, clip_ref[f, p], (((1,), (1,)), ((), ())), preferred_element_type=F32
            )
            x[f, p] = (ranked * kept).astype(BF16)
            return carry

        lax.fori_loop(0, positions, place, 0, unroll=4)
        return carry

    lax.fori_loop(0, most_ref[0], load, 0)

    for layer in range(layers):
        rows = depth_ref[layer].astype(F32)
        for t in range(tap_count):
            taps[layer, t] = jnp.broadcast_to(rows[t : t + 1], (ROWS, expanded)).astype(BF16)

    lanes = [(at, min(at + 128, expanded)) for at in range(0, expanded, 128)]

    def convolve(layer, f, shifts):
        for lo, hi in lanes:
            for y in range(SIDE):
                sums = [None] * SIDE
                for a in shifts:
                    for b in range(3):
                        if not 0 <= y + b - 1 < SIDE:
                            continue
                        line = [
                            hidden[f + a - 1, (y + b - 1) * SIDE + z, :, lo:hi]
                            for z in range(SIDE)
                        ]
                        weights = [taps[layer, 9 * a + 3 * b + g, :, lo:hi] for g in range(3)]
                        for z in range(SIDE):
                            for g in range(3):
                                if 0 <= z + g - 1 < SIDE:
                                    term = weights[g] * line[z + g - 1]
                                    sums[z] = term if sums[z] is None else sums[z] + term
                for z in range(SIDE):
                    half = 0.5 * sums[z].astype(F32)
                    activated[y * SIDE + z, :, lo:hi] = (half + half * jnp.tanh(half)).astype(BF16)

    def block(b, carry):
        most = most_ref[b]
        first = pl.multiple_of(b * ROWS, ROWS)
        counts = count_ref[pl.ds(first, ROWS), :]

        def mask(f, width):
            wide = jnp.broadcast_to(counts, (ROWS, width))
            return jnp.where(wide > f.astype(F32), 1.0, 0.0)

        def layer_step(layer, carry):
            def expand(f, carry):
                wide = jnp.dot(
                    x[f, :, pl.ds(first, ROWS), :].reshape(flat, channels), expand_ref[layer], preferred_element_type=F32
                )
                wide = jnp.maximum(wide, 0.0).astype(BF16).reshape(positions, ROWS, expanded)
                hidden[f] = wide * mask(f, expanded).astype(BF16)[None]
                return carry

            lax.fori_loop(0, most, expand, 0)

            def mix(f, carry):
                has_last, has_next = f > 0, f < most - 1
                for last in (False, True):
                    for following in (False, True):
                        shifts = ([0] if last else []) + [1] + ([2] if following else [])
                        chosen = jnp.logical_and(has_last == last, has_next == following)
                        pl.when(chosen)(functools.partial(convolve, layer, f, shifts))
                branch = jnp.dot(
                    activated[...].reshape(flat, expanded),
                    reduce_ref[layer],
                    preferred_element_type=F32,
                ).reshape(positions, ROWS, channels)
                kept = x[f, :, pl.ds(first, ROWS), :].astype(F32)
                x[f, :, pl.ds(first, ROWS), :] = (
                    kept + branch * mask(f, channels)[None]
                ).astype(BF16)
                return carry

            lax.fori_loop(0, most, mix, 0)
            return carry

        lax.fori_loop(0, layers, layer_step, 0)

        total = lax.fori_loop(
            0,
            most,
            lambda f, total: total + jnp.sum(x[f, :, pl.ds(first, ROWS), :].astype(F32), axis=0),
            jnp.zeros((ROWS, channels), F32),
        )
        mean = total / (jnp.broadcast_to(counts, (ROWS, channels)) * positions)
        pooled[pl.ds(first, ROWS), :] = mean.astype(BF16)
        return carry

    lax.fori_loop(0, blocks, block, 0)

    projected = jnp.dot(pooled[...], head_ref[...], preferred_element_type=F32)
    square = jnp.sum(projected * projected, axis=1, keepdims=True)
    vectors = (projected * lax.rsqrt(square + 1e-06)).astype(BF16)
    slots = lax.broadcasted_iota(jnp.int32, (clips, clips), 0)
    chosen = jnp.where(slots == place_ref[...], 1.0, 0.0).astype(BF16)
    out_ref[...] = jnp.dot(chosen, vectors, preferred_element_type=F32).astype(BF16)


def embed(clip_data, counts, places, expand_weight, depth_kernel, reduce_weight, head_weight):
    clips, frames, positions, channels = clip_data.shape
    layers, tap_count, expanded = depth_kernel.shape
    slots = jnp.arange(clips, dtype=jnp.int32)
    ahead = (counts[None, :] > counts[:, None]) | (
        (counts[None, :] == counts[:, None]) & (slots[None, :] < slots[:, None])
    )
    rank = jnp.sum(ahead.astype(jnp.int32), axis=1)
    at_rank = rank[None, :] == slots[:, None]

    def ranked(values):
        return jnp.sum(jnp.where(at_rank, values[None, :], 0), axis=1)

    order, sorted_counts, sorted_places = ranked(slots), ranked(counts), ranked(places)
    vmem = pl.BlockSpec(memory_space=pltpu.VMEM)
    smem = pl.BlockSpec(memory_space=pltpu.SMEM)
    return pl.pallas_call(
        embed_kernel,
        out_shape=jax.ShapeDtypeStruct((clips, head_weight.shape[1]), BF16),
        in_specs=[smem] + [vmem] * 8,
        out_specs=vmem,
        scratch_shapes=[
            pltpu.VMEM((frames, positions, clips, channels), BF16),
            pltpu.VMEM((frames, positions, ROWS, expanded), BF16),
            pltpu.VMEM((positions, ROWS, expanded), BF16),
            pltpu.VMEM((clips, channels), BF16),
            pltpu.VMEM((layers, tap_count, ROWS, expanded), BF16),
        ],
        compiler_params=pltpu.CompilerParams(vmem_limit_bytes=40 << 20),
        name="embed_clips",
    )(
        sorted_counts[::ROWS],
        order[:, None],
        clip_data.transpose(1, 2, 3, 0),
        sorted_counts.astype(F32)[:, None],
        sorted_places[None, :],
        expand_weight,
        depth_kernel,
        reduce_weight,
        head_weight,
    )


def score_kernel(panel_size, known, part, rows_ref, label_ref, panel_ref, out_ref, best):
    step, final = pl.program_id(0), pl.num_programs(0) - 1
    tile = panel_ref.shape[0]
    rows = rows_ref.shape[0]

    @pl.when(step == 0)
    def _():
        best[...] = jnp.full(best.shape, -jnp.inf, F32)

    for at in range(0, tile, part):
        scores = lax.dot_general(
            panel_ref[at : at + part, :],
            rows_ref[...],
            (((1,), (1,)), ((), ())),
            preferred_element_type=F32,
        )
        if at == 0:

            @pl.when(step == 0)
            def _():
                index = lax.broadcasted_iota(jnp.int32, (known, rows), 0)
                own = jnp.where(index == label_ref[...], scores[:known], -jnp.inf)
                out_ref[1:2, :] = jnp.max(own, axis=0, keepdims=True)

        def keep(values):
            best[...] = jnp.maximum(best[...], jnp.max(values.reshape(part // 8, 8, rows), axis=0))

        @pl.when(step < final)
        def _():
            keep(scores)

        @pl.when(step == final)
        def _():
            place = step * tile + at + lax.broadcasted_iota(jnp.int32, scores.shape, 0)
            keep(jnp.where(place < panel_size, scores, -jnp.inf))

    @pl.when(step == pl.num_programs(0) - 1)
    def _():
        out_ref[0:1, :] = jnp.max(best[...], axis=0, keepdims=True)


def panel_scores(rows, labels, centroids, known):
    panel_size, width = centroids.shape
    count = rows.shape[0]
    tile, part = 1024, 256
    return pl.pallas_call(
        functools.partial(score_kernel, panel_size, known, part),
        out_shape=jax.ShapeDtypeStruct((2, count), F32),
        grid=(pl.cdiv(panel_size, tile),),
        in_specs=[
            pl.BlockSpec((count, width), lambda i: (0, 0)),
            pl.BlockSpec((1, count), lambda i: (0, 0)),
            pl.BlockSpec((tile, width), lambda i: (i, 0)),
        ],
        out_specs=pl.BlockSpec((2, count), lambda i: (0, 0)),
        scratch_shapes=[pltpu.VMEM((8, count), F32)],
        compiler_params=pltpu.CompilerParams(vmem_limit_bytes=40 << 20),
        name="panel_scores",
    )(rows, labels, centroids)


def exchange_kernel(
    n_dp,
    n_cent,
    outgoing_ref,
    seat_ref,
    vectors_ref,
    rows_ref,
    members_ref,
    landed,
    rows,
    leaving,
    members,
    shuffle_send,
    shuffle_recv,
    gather_send,
    gather_recv,
    member_send,
    member_recv,
):
    dp, cent = lax.axis_index("dp"), lax.axis_index("cent")
    per_peer, width = outgoing_ref.shape[1:]
    clips = n_dp * per_peer
    seats = members.shape[2]
    mesh_id = pl.DeviceIdType.MESH
    chips = n_cent // 2
    chip, core = cent // 2, cent % 2

    barrier = pltpu.get_barrier_semaphore()
    for s in range(1, n_dp):
        pl.semaphore_signal(
            barrier, inc=1, device_id=((dp + s) % n_dp, cent), device_id_type=mesh_id
        )
    for s in range(1, n_cent):
        pl.semaphore_signal(
            barrier, inc=1, device_id=(dp, (cent + s) % n_cent), device_id_type=mesh_id
        )
    pl.semaphore_wait(barrier, n_dp + n_cent - 2)

    shuffles = []
    for s in range(1, n_dp):
        peer = (dp + s) % n_dp
        copy = pltpu.make_async_remote_copy(
            src_ref=outgoing_ref.at[peer],
            dst_ref=landed.at[dp],
            send_sem=shuffle_send.at[s],
            recv_sem=shuffle_recv.at[s],
            device_id=(peer, cent),
            device_id_type=mesh_id,
        )
        copy.start()
        shuffles.append(copy)
    landed[dp] = outgoing_ref[dp]
    for copy in shuffles:
        copy.wait()

    to_row = lax.broadcasted_iota(jnp.int32, (clips, clips), 0)
    from_row = lax.broadcasted_iota(jnp.int32, (clips, clips), 1)
    turn = jnp.where(from_row == to_row % n_dp * per_peer + to_row // n_dp, 1.0, 0.0)
    vectors = jnp.dot(
        turn.astype(BF16), landed[...].reshape(clips, width), preferred_element_type=F32
    ).astype(BF16)
    vectors_ref[...] = vectors
    rows[cent] = vectors

    gathers, sources = [None], [cent]
    for i in range(1, n_cent):
        hop, side = i // 2, i % 2
        sources.append((chip + hop) % chips * 2 + (core + side) % 2)
        copy = pltpu.make_async_remote_copy(
            src_ref=rows.at[cent],
            dst_ref=rows.at[cent],
            send_sem=gather_send.at[i],
            recv_sem=gather_recv.at[i],
            device_id=(dp, (chip + chips - hop) % chips * 2 + (core + side) % 2),
            device_id_type=mesh_id,
        )
        copy.start()
        gathers.append(copy)

    seat_of = lax.broadcasted_iota(jnp.int32, (n_dp * seats, clips), 0)
    handed = []
    for i, source in enumerate(sources):
        if i:
            gathers[i].wait_recv()
        chosen = jnp.where(seat_of == seat_ref[source], 1.0, 0.0).astype(BF16)
        seated = jnp.dot(chosen, rows[source], preferred_element_type=F32).astype(BF16)
        leaving[i] = seated.reshape(n_dp, seats, width)
        for s in range(1, n_dp):
            peer = (dp + s) % n_dp
            copy = pltpu.make_async_remote_copy(
                src_ref=leaving.at[i, peer],
                dst_ref=members.at[dp, source],
                send_sem=member_send.at[i, s],
                recv_sem=member_recv.at[i, s],
                device_id=(peer, cent),
                device_id_type=mesh_id,
            )
            copy.start()
            handed.append(copy)
        members[dp, source] = leaving[i, dp]
    for copy in gathers[1:]:
        copy.wait_send()
    rows_ref[...] = rows[...]
    for copy in handed:
        copy.wait()
    members_ref[...] = members[...]


def exchange(outgoing, seat_of_row, n_dp, n_cent, seats):
    per_peer, width = outgoing.shape[1:]
    clips = n_dp * per_peer
    vmem = pl.BlockSpec(memory_space=pltpu.VMEM)
    dma = pltpu.SemaphoreType.DMA
    return pl.pallas_call(
        functools.partial(exchange_kernel, n_dp, n_cent),
        out_shape=(
            jax.ShapeDtypeStruct((clips, width), BF16),
            jax.ShapeDtypeStruct((n_cent, clips, width), BF16),
            jax.ShapeDtypeStruct((n_dp, n_cent, seats, width), BF16),
        ),
        in_specs=[vmem] * 2,
        out_specs=(vmem,) * 3,
        scratch_shapes=[
            pltpu.VMEM((n_dp, per_peer, width), BF16),
            pltpu.VMEM((n_cent, clips, width), BF16),
            pltpu.VMEM((n_cent, n_dp, seats, width), BF16),
            pltpu.VMEM((n_dp, n_cent, seats, width), BF16),
            dma((n_dp,)),
            dma((n_dp,)),
            dma((n_cent,)),
            dma((n_cent,)),
            dma((n_cent, n_dp)),
            dma((n_cent, n_dp)),
        ],
        compiler_params=pltpu.CompilerParams(
            collective_id=0, has_side_effects=True, vmem_limit_bytes=40 << 20
        ),
        name="exchange",
    )(outgoing, seat_of_row)


def local(
    clip_data,
    frame_counts,
    send_list,
    cluster_ids,
    expand_weight,
    depth_kernel,
    reduce_weight,
    head_weight,
    centroids,
):
    n_dp = lax.axis_size("dp")
    n_cent = lax.axis_size("cent")
    both = ("dp", "cent")
    clip_count = clip_data.shape[0]
    panel_size = centroids.shape[0]
    per_peer = clip_count // n_dp
    owner_total = n_dp * n_cent
    capacity = max(ROWS, 4 * clip_count // owner_total)
    slot_total = owner_total * capacity
    me = lax.axis_index("dp") * n_cent + lax.axis_index("cent")

    def owner_of(ids):
        return ids % panel_size % n_dp * n_cent + ids // panel_size

    every_id = lax.all_gather(cluster_ids[0], both, axis=0)
    group_ids = lax.dynamic_slice_in_dim(
        every_id, lax.axis_index("dp") * n_cent, n_cent, axis=0
    ).reshape(n_cent, clip_count)
    here = group_ids // panel_size == lax.axis_index("cent")
    labels = jnp.where(here, group_ids % panel_size, -1).reshape(1, n_cent * clip_count)
    mine = owner_of(every_id) == me
    slots = jnp.arange(clip_count, dtype=jnp.int32)
    before = (slots[:, None] < slots[None, :]).astype(BF16)
    rank_here = jnp.dot(mine.astype(BF16), before, preferred_element_type=F32).astype(jnp.int32)
    seats = jnp.arange(capacity, dtype=jnp.int32)
    seated = mine[:, None, :] & (rank_here[:, None, :] == seats[None, :, None])
    member_ids = (
        jnp.sum(jnp.where(seated, every_id[:, None, :] + 1, 0), axis=2).reshape(slot_total) - 1
    )

    target = jnp.where(here, group_ids % panel_size % n_dp, -1)
    earlier = (target[:, :, None] == target[:, None, :]) & (slots[:, None] < slots[None, :])
    seat = target * capacity + jnp.sum(earlier.astype(jnp.int32), axis=1)
    seat = jnp.where(here, seat, -1)
    places = send_list[0] % n_dp * per_peer + send_list[0] // n_dp

    outgoing = embed(
        clip_data,
        frame_counts[0],
        places,
        expand_weight,
        depth_kernel,
        reduce_weight,
        head_weight,
    )
    width = outgoing.shape[1]
    vectors, block_rows, members = exchange(
        outgoing.reshape(n_dp, per_peer, width), seat[:, None, :], n_dp, n_cent, capacity
    )
    block_rows = block_rows.reshape(n_cent * clip_count, width)
    members = members.reshape(slot_total, width)
    similarity = jnp.einsum("rd,td->rt", members, members, preferred_element_type=F32)
    index = jnp.arange(slot_total, dtype=jnp.int32)
    same_cluster = (
        (member_ids[:, None] == member_ids[None, :])
        & (member_ids >= 0)[:, None]
        & (index[:, None] != index[None, :])
    )
    peer_values = jnp.max(jnp.where(same_cluster, similarity, -1.0), axis=1)
    back = lax.all_to_all(
        peer_values.reshape(n_dp, n_cent, capacity),
        "dp",
        split_axis=0,
        concat_axis=0,
        tiled=True,
    )
    back = back.transpose(1, 0, 2).reshape(n_cent, n_dp * capacity)
    at_seat = jnp.arange(n_dp * capacity, dtype=jnp.int32)[None, :, None] == seat[:, None, :]
    peers = jnp.max(jnp.where(at_seat, back[:, :, None], -1.0), axis=1)
    scored = panel_scores(block_rows, labels, centroids, GROUPS * n_dp)
    partial = jnp.concatenate([scored.reshape(2, n_cent, clip_count), peers[None]], axis=0)
    partial = lax.all_to_all(
        partial.transpose(1, 0, 2), "cent", split_axis=0, concat_axis=0, tiled=True
    )
    nearest, own_sim, peer_sim = jnp.max(partial, axis=0)
    return (vectors, nearest, own_sim, peer_sim)


def solution(mesh):
    placed = (
        P(("dp", "cent"), None, None, None),
        P(("dp", "cent"), None),
        P(("dp", "cent"), None),
        P(("dp", "cent"), None),
        P(),
        P(),
        P(),
        P(),
        P("cent", None),
    )
    return jax.shard_map(
        local,
        mesh=mesh,
        in_specs=placed,
        out_specs=(
            P(("dp", "cent"), None),
            P(("dp", "cent")),
            P(("dp", "cent")),
            P(("dp", "cent")),
        ),
        check_vma=False,
    )
```

```python
import functools

import jax
import jax.numpy as jnp
from jax import lax
from jax.experimental import pallas as pl
from jax.experimental.pallas import tpu as pltpu
from jax.sharding import PartitionSpec as P

SIDE = 4
GROUPS = 4
ROWS = 16
F32 = jnp.float32
BF16 = jnp.bfloat16


def embed_kernel(
    most_ref,
    order_ref,
    clip_ref,
    count_ref,
    place_ref,
    expand_ref,
    depth_ref,
    reduce_ref,
    head_ref,
    out_ref,
    x,
    hidden,
    activated,
    pooled,
    taps,
):
    frames, positions, channels, clips = clip_ref.shape
    layers, tap_count, expanded = depth_ref.shape
    blocks = clips // ROWS
    flat = positions * ROWS

    clip_of = lax.broadcasted_iota(jnp.int32, (clips, clips), 1)
    by_count = jnp.where(clip_of == order_ref[...], 1.0, 0.0).astype(BF16)
    every_count = jnp.broadcast_to(count_ref[...], (clips, channels))

    def load(f, carry):
        kept = jnp.where(every_count > f.astype(F32), 1.0, 0.0)

        def place(p, carry):
            ranked = lax.dot_general(
                by_count, clip_ref[f, p], (((1,), (1,)), ((), ())), preferred_element_type=F32
            )
            x[f, p] = (ranked * kept).astype(BF16)
            return carry

        lax.fori_loop(0, positions, place, 0, unroll=4)
        return carry

    lax.fori_loop(0, most_ref[0], load, 0)

    for layer in range(layers):
        rows = depth_ref[layer].astype(F32)
        for t in range(tap_count):
            taps[layer, t] = jnp.broadcast_to(rows[t : t + 1], (ROWS, expanded)).astype(BF16)

    lanes = [(at, min(at + 128, expanded)) for at in range(0, expanded, 128)]

    def convolve(layer, f, shifts):
        for lo, hi in lanes:
            for y in range(SIDE):
                sums = [None] * SIDE
                for a in shifts:
                    for b in range(3):
                        if not 0 <= y + b - 1 < SIDE:
                            continue
                        line = [
                            hidden[f + a - 1, (y + b - 1) * SIDE + z, :, lo:hi]
                            for z in range(SIDE)
                        ]
                        weights = [taps[layer, 9 * a + 3 * b + g, :, lo:hi] for g in range(3)]
                        for z in range(SIDE):
                            for g in range(3):
                                if 0 <= z + g - 1 < SIDE:
                                    term = weights[g] * line[z + g - 1]
                                    sums[z] = term if sums[z] is None else sums[z] + term
                for z in range(SIDE):
                    half = 0.5 * sums[z].astype(F32)
                    activated[y * SIDE + z, :, lo:hi] = (half + half * jnp.tanh(half)).astype(BF16)

    def block(b, carry):
        most = most_ref[b]
        first = pl.multiple_of(b * ROWS, ROWS)
        counts = count_ref[pl.ds(first, ROWS), :]

        def mask(f, width):
            wide = jnp.broadcast_to(counts, (ROWS, width))
            return jnp.where(wide > f.astype(F32), 1.0, 0.0)

        def layer_step(layer, carry):
            def expand(f, carry):
                wide = jnp.dot(
                    x[f, :, pl.ds(first, ROWS), :].reshape(flat, channels), expand_ref[layer], preferred_element_type=F32
                )
                wide = jnp.maximum(wide, 0.0).astype(BF16).reshape(positions, ROWS, expanded)
                hidden[f] = wide * mask(f, expanded).astype(BF16)[None]
                return carry

            lax.fori_loop(0, most, expand, 0)

            def mix(f, carry):
                has_last, has_next = f > 0, f < most - 1
                for last in (False, True):
                    for following in (False, True):
                        shifts = ([0] if last else []) + [1] + ([2] if following else [])
                        chosen = jnp.logical_and(has_last == last, has_next == following)
                        pl.when(chosen)(functools.partial(convolve, layer, f, shifts))
                branch = jnp.dot(
                    activated[...].reshape(flat, expanded),
                    reduce_ref[layer],
                    preferred_element_type=F32,
                ).reshape(positions, ROWS, channels)
                kept = x[f, :, pl.ds(first, ROWS), :].astype(F32)
                x[f, :, pl.ds(first, ROWS), :] = (
                    kept + branch * mask(f, channels)[None]
                ).astype(BF16)
                return carry

            lax.fori_loop(0, most, mix, 0)
            return carry

        lax.fori_loop(0, layers, layer_step, 0)

        total = lax.fori_loop(
            0,
            most,
            lambda f, total: total + jnp.sum(x[f, :, pl.ds(first, ROWS), :].astype(F32), axis=0),
            jnp.zeros((ROWS, channels), F32),
        )
        mean = total / (jnp.broadcast_to(counts, (ROWS, channels)) * positions)
        pooled[pl.ds(first, ROWS), :] = mean.astype(BF16)
        return carry

    lax.fori_loop(0, blocks, block, 0)

    projected = jnp.dot(pooled[...], head_ref[...], preferred_element_type=F32)
    square = jnp.sum(projected * projected, axis=1, keepdims=True)
    vectors = (projected * lax.rsqrt(square + 1e-06)).astype(BF16)
    slots = lax.broadcasted_iota(jnp.int32, (clips, clips), 0)
    chosen = jnp.where(slots == place_ref[...], 1.0, 0.0).astype(BF16)
    out_ref[...] = jnp.dot(chosen, vectors, preferred_element_type=F32).astype(BF16)


def embed(clip_data, counts, places, expand_weight, depth_kernel, reduce_weight, head_weight):
    clips, frames, positions, channels = clip_data.shape
    layers, tap_count, expanded = depth_kernel.shape
    slots = jnp.arange(clips, dtype=jnp.int32)
    ahead = (counts[None, :] > counts[:, None]) | (
        (counts[None, :] == counts[:, None]) & (slots[None, :] < slots[:, None])
    )
    rank = jnp.sum(ahead.astype(jnp.int32), axis=1)
    at_rank = rank[None, :] == slots[:, None]

    def ranked(values):
        return jnp.sum(jnp.where(at_rank, values[None, :], 0), axis=1)

    order, sorted_counts, sorted_places = ranked(slots), ranked(counts), ranked(places)
    vmem = pl.BlockSpec(memory_space=pltpu.VMEM)
    smem = pl.BlockSpec(memory_space=pltpu.SMEM)
    return pl.pallas_call(
        embed_kernel,
        out_shape=jax.ShapeDtypeStruct((clips, head_weight.shape[1]), BF16),
        in_specs=[smem] + [vmem] * 8,
        out_specs=vmem,
        scratch_shapes=[
            pltpu.VMEM((frames, positions, clips, channels), BF16),
            pltpu.VMEM((frames, positions, ROWS, expanded), BF16),
            pltpu.VMEM((positions, ROWS, expanded), BF16),
            pltpu.VMEM((clips, channels), BF16),
            pltpu.VMEM((layers, tap_count, ROWS, expanded), BF16),
        ],
        compiler_params=pltpu.CompilerParams(vmem_limit_bytes=40 << 20),
        name="embed_clips",
    )(
        sorted_counts[::ROWS],
        order[:, None],
        clip_data.transpose(1, 2, 3, 0),
        sorted_counts.astype(F32)[:, None],
        sorted_places[None, :],
        expand_weight,
        depth_kernel,
        reduce_weight,
        head_weight,
    )


def score_kernel(panel_size, known, part, rows_ref, label_ref, panel_ref, out_ref, best):
    step = pl.program_id(0)
    tile = panel_ref.shape[0]
    rows = rows_ref.shape[0]

    @pl.when(step == 0)
    def _():
        best[...] = jnp.full(best.shape, -jnp.inf, F32)

    for at in range(0, tile, part):
        scores = lax.dot_general(
            panel_ref[at : at + part, :],
            rows_ref[...],
            (((1,), (1,)), ((), ())),
            preferred_element_type=F32,
        )
        if at == 0:

            @pl.when(step == 0)
            def _():
                index = lax.broadcasted_iota(jnp.int32, (known, rows), 0)
                own = jnp.where(index == label_ref[...], scores[:known], -jnp.inf)
                out_ref[1:2, :] = jnp.max(own, axis=0, keepdims=True)

        place = step * tile + at + lax.broadcasted_iota(jnp.int32, scores.shape, 0)
        scores = jnp.where(place < panel_size, scores, -jnp.inf)
        best[...] = jnp.maximum(best[...], jnp.max(scores.reshape(part // 8, 8, rows), axis=0))

    @pl.when(step == pl.num_programs(0) - 1)
    def _():
        out_ref[0:1, :] = jnp.max(best[...], axis=0, keepdims=True)


def panel_scores(rows, labels, centroids, known):
    panel_size, width = centroids.shape
    count = rows.shape[0]
    tile, part = 1024, 256
    return pl.pallas_call(
        functools.partial(score_kernel, panel_size, known, part),
        out_shape=jax.ShapeDtypeStruct((2, count), F32),
        grid=(pl.cdiv(panel_size, tile),),
        in_specs=[
            pl.BlockSpec((count, width), lambda i: (0, 0)),
            pl.BlockSpec((1, count), lambda i: (0, 0)),
            pl.BlockSpec((tile, width), lambda i: (i, 0)),
        ],
        out_specs=pl.BlockSpec((2, count), lambda i: (0, 0)),
        scratch_shapes=[pltpu.VMEM((8, count), F32)],
        compiler_params=pltpu.CompilerParams(vmem_limit_bytes=40 << 20),
        name="panel_scores",
    )(rows, labels, centroids)


def exchange_kernel(
    n_dp,
    n_cent,
    outgoing_ref,
    seat_ref,
    vectors_ref,
    rows_ref,
    members_ref,
    landed,
    rows,
    leaving,
    members,
    shuffle_send,
    shuffle_recv,
    gather_send,
    gather_recv,
    member_send,
    member_recv,
):
    dp, cent = lax.axis_index("dp"), lax.axis_index("cent")
    per_peer, width = outgoing_ref.shape[1:]
    clips = n_dp * per_peer
    seats = members.shape[2]
    mesh_id = pl.DeviceIdType.MESH
    chips = n_cent // 2
    chip, core = cent // 2, cent % 2

    barrier = pltpu.get_barrier_semaphore()
    for s in range(1, n_dp):
        pl.semaphore_signal(
            barrier, inc=1, device_id=((dp + s) % n_dp, cent), device_id_type=mesh_id
        )
    for s in range(1, n_cent):
        pl.semaphore_signal(
            barrier, inc=1, device_id=(dp, (cent + s) % n_cent), device_id_type=mesh_id
        )
    pl.semaphore_wait(barrier, n_dp + n_cent - 2)

    shuffles = []
    for s in range(1, n_dp):
        peer = (dp + s) % n_dp
        copy = pltpu.make_async_remote_copy(
            src_ref=outgoing_ref.at[peer],
            dst_ref=landed.at[dp],
            send_sem=shuffle_send.at[s],
            recv_sem=shuffle_recv.at[s],
            device_id=(peer, cent),
            device_id_type=mesh_id,
        )
        copy.start()
        shuffles.append(copy)
    landed[dp] = outgoing_ref[dp]
    for copy in shuffles:
        copy.wait()

    to_row = lax.broadcasted_iota(jnp.int32, (clips, clips), 0)
    from_row = lax.broadcasted_iota(jnp.int32, (clips, clips), 1)
    turn = jnp.where(from_row == to_row % n_dp * per_peer + to_row // n_dp, 1.0, 0.0)
    vectors = jnp.dot(
        turn.astype(BF16), landed[...].reshape(clips, width), preferred_element_type=F32
    ).astype(BF16)
    vectors_ref[...] = vectors
    rows[cent] = vectors

    gathers, sources = [None], [cent]
    for i in range(1, n_cent):
        hop, side = i // 2, i % 2
        sources.append((chip + hop) % chips * 2 + (core + side) % 2)
        copy = pltpu.make_async_remote_copy(
            src_ref=rows.at[cent],
            dst_ref=rows.at[cent],
            send_sem=gather_send.at[i],
            recv_sem=gather_recv.at[i],
            device_id=(dp, (chip + chips - hop) % chips * 2 + (core + side) % 2),
            device_id_type=mesh_id,
        )
        copy.start()
        gathers.append(copy)

    seat_of = lax.broadcasted_iota(jnp.int32, (n_dp * seats, clips), 0)
    handed = []
    for i, source in enumerate(sources):
        if i:
            gathers[i].wait_recv()
        chosen = jnp.where(seat_of == seat_ref[source], 1.0, 0.0).astype(BF16)
        seated = jnp.dot(chosen, rows[source], preferred_element_type=F32).astype(BF16)
        leaving[i] = seated.reshape(n_dp, seats, width)
        for s in range(1, n_dp):
            peer = (dp + s) % n_dp
            copy = pltpu.make_async_remote_copy(
                src_ref=leaving.at[i, peer],
                dst_ref=members.at[dp, source],
                send_sem=member_send.at[i, s],
                recv_sem=member_recv.at[i, s],
                device_id=(peer, cent),
                device_id_type=mesh_id,
            )
            copy.start()
            handed.append(copy)
        members[dp, source] = leaving[i, dp]
    for copy in gathers[1:]:
        copy.wait_send()
    rows_ref[...] = rows[...]
    for copy in handed:
        copy.wait()
    members_ref[...] = members[...]


def exchange(outgoing, seat_of_row, n_dp, n_cent, seats):
    per_peer, width = outgoing.shape[1:]
    clips = n_dp * per_peer
    vmem = pl.BlockSpec(memory_space=pltpu.VMEM)
    dma = pltpu.SemaphoreType.DMA
    return pl.pallas_call(
        functools.partial(exchange_kernel, n_dp, n_cent),
        out_shape=(
            jax.ShapeDtypeStruct((clips, width), BF16),
            jax.ShapeDtypeStruct((n_cent, clips, width), BF16),
            jax.ShapeDtypeStruct((n_dp, n_cent, seats, width), BF16),
        ),
        in_specs=[vmem] * 2,
        out_specs=(vmem,) * 3,
        scratch_shapes=[
            pltpu.VMEM((n_dp, per_peer, width), BF16),
            pltpu.VMEM((n_cent, clips, width), BF16),
            pltpu.VMEM((n_cent, n_dp, seats, width), BF16),
            pltpu.VMEM((n_dp, n_cent, seats, width), BF16),
            dma((n_dp,)),
            dma((n_dp,)),
            dma((n_cent,)),
            dma((n_cent,)),
            dma((n_cent, n_dp)),
            dma((n_cent, n_dp)),
        ],
        compiler_params=pltpu.CompilerParams(
            collective_id=0, has_side_effects=True, vmem_limit_bytes=40 << 20
        ),
        name="exchange",
    )(outgoing, seat_of_row)


def local(
    clip_data,
    frame_counts,
    send_list,
    cluster_ids,
    expand_weight,
    depth_kernel,
    reduce_weight,
    head_weight,
    centroids,
):
    n_dp = lax.axis_size("dp")
    n_cent = lax.axis_size("cent")
    both = ("dp", "cent")
    clip_count = clip_data.shape[0]
    panel_size = centroids.shape[0]
    per_peer = clip_count // n_dp
    owner_total = n_dp * n_cent
    capacity = max(ROWS, 4 * clip_count // owner_total)
    slot_total = owner_total * capacity
    me = lax.axis_index("dp") * n_cent + lax.axis_index("cent")

    def owner_of(ids):
        return ids % panel_size % n_dp * n_cent + ids // panel_size

    every_id = lax.all_to_all(
        jnp.broadcast_to(cluster_ids, (owner_total, clip_count)),
        both,
        split_axis=0,
        concat_axis=0,
        tiled=True,
    )
    group_ids = lax.dynamic_slice_in_dim(
        every_id, lax.axis_index("dp") * n_cent, n_cent, axis=0
    ).reshape(n_cent, clip_count)
    here = group_ids // panel_size == lax.axis_index("cent")
    labels = jnp.where(here, group_ids % panel_size, -1).reshape(1, n_cent * clip_count)
    mine = owner_of(every_id) == me
    slots = jnp.arange(clip_count, dtype=jnp.int32)
    before = (slots[:, None] < slots[None, :]).astype(BF16)
    rank_here = jnp.dot(mine.astype(BF16), before, preferred_element_type=F32).astype(jnp.int32)
    seats = jnp.arange(capacity, dtype=jnp.int32)
    seated = mine[:, None, :] & (rank_here[:, None, :] == seats[None, :, None])
    member_ids = (
        jnp.sum(jnp.where(seated, every_id[:, None, :] + 1, 0), axis=2).reshape(slot_total) - 1
    )

    target = jnp.where(here, group_ids % panel_size % n_dp, -1)
    earlier = (target[:, :, None] == target[:, None, :]) & (slots[:, None] < slots[None, :])
    seat = target * capacity + jnp.sum(earlier.astype(jnp.int32), axis=1)
    seat = jnp.where(here, seat, -1)
    places = send_list[0] % n_dp * per_peer + send_list[0] // n_dp

    outgoing = embed(
        clip_data,
        frame_counts[0],
        places,
        expand_weight,
        depth_kernel,
        reduce_weight,
        head_weight,
    )
    width = outgoing.shape[1]
    vectors, block_rows, members = exchange(
        outgoing.reshape(n_dp, per_peer, width), seat[:, None, :], n_dp, n_cent, capacity
    )
    block_rows = block_rows.reshape(n_cent * clip_count, width)
    members = members.reshape(slot_total, width)
    similarity = jnp.einsum("rd,td->rt", members, members, preferred_element_type=F32)
    index = jnp.arange(slot_total, dtype=jnp.int32)
    same_cluster = (
        (member_ids[:, None] == member_ids[None, :])
        & (member_ids >= 0)[:, None]
        & (index[:, None] != index[None, :])
    )
    peer_values = jnp.max(jnp.where(same_cluster, similarity, -1.0), axis=1)
    back = lax.all_to_all(
        peer_values.reshape(n_dp, n_cent, capacity),
        "dp",
        split_axis=0,
        concat_axis=0,
        tiled=True,
    )
    back = back.transpose(1, 0, 2).reshape(n_cent, n_dp * capacity)
    at_seat = jnp.arange(n_dp * capacity, dtype=jnp.int32)[None, :, None] == seat[:, None, :]
    peers = jnp.max(jnp.where(at_seat, back[:, :, None], -1.0), axis=1)
    scored = panel_scores(block_rows, labels, centroids, GROUPS * n_dp)
    partial = jnp.concatenate([scored.reshape(2, n_cent, clip_count), peers[None]], axis=0)
    partial = lax.all_to_all(
        partial.transpose(1, 0, 2), "cent", split_axis=0, concat_axis=0, tiled=True
    )
    nearest, own_sim, peer_sim = jnp.max(partial, axis=0)
    return (vectors, nearest, own_sim, peer_sim)


def solution(mesh):
    placed = (
        P(("dp", "cent"), None, None, None),
        P(("dp", "cent"), None),
        P(("dp", "cent"), None),
        P(("dp", "cent"), None),
        P(),
        P(),
        P(),
        P(),
        P("cent", None),
    )
    return jax.shard_map(
        local,
        mesh=mesh,
        in_specs=placed,
        out_specs=(
            P(("dp", "cent"), None),
            P(("dp", "cent")),
            P(("dp", "cent")),
            P(("dp", "cent")),
        ),
        check_vma=False,
    )
```
